32 devices in a mesh: groups: 2 (over x), row: 4 (over z), col: 4 (over y, core).
Axes of the slice: x: 2, y: 2, z: 4, core: 2. Of those that a mesh axis runs over, the one named last changes fastest.
Arguments:
- height: float32 [4096, 1024], P(('groups', 'row'), 'col'), parts along dimension 0, may hold values from -2.5 to 2.5
- rigidity: float32 [4096, 1024], P(('groups', 'row'), 'col'), parts along dimension 0, may hold values from 0.4 to 1.6
- adhesion: float32 [4096, 1024], P(('groups', 'row'), 'col'), parts along dimension 0, may hold values from 1 to 10
- forcing: bfloat16 [4, 4096, 1024], P(None, ('groups', 'row'), 'col'), parts along dimension 1, may hold values from -6 to 6
Outputs:
- new_height: float32 [4096, 1024], P(('groups', 'row'), 'col'), parts along dimension 0
- velocity_spectrum: float32 [2048, 2, 1024], P(('groups', 'col'), None, 'row'), parts along dimension 0
The draws below stay inside these ranges and needn't reach their ends.
There are 2 independent parts, one for each index of `groups`. The reference program is written for one: setup_inputs(seed, part) draws one part's arguments, and reference() takes and returns one part's arrays. A program takes and returns all parts, laid end to end along the dimension named above; each array names one. Nothing has to cross between parts.
All inputs are finite; a program needn't handle non-finite values.
Results may differ from the reference program's by a relative error of at most 0.0067.
Values may be sent and summed in bfloat16 or wider, within the bound.
A program may use at most 128 MiB of HBM per device.

```python
import math
import jax
import jax.numpy as jnp
from jax import lax

CC = 256
SUB = 4
NX = 2048
NY = 1024
KX = 1024


def block_scale(own_key, shape, split, smallest, top_value):
    gain, own = 1.0, jax.random.fold_in(own_key, 6)
    for axis_at, blocks in split:
        heights = jnp.exp(jax.random.uniform(jax.random.fold_in(own, axis_at), (blocks,), jnp.float32, smallest / len(split), top_value / len(split)))
        gain = gain * jnp.repeat(heights, shape[axis_at] // blocks).reshape([-1 if axis == axis_at else 1 for axis in range(len(shape))])
    return gain


def bell_draw(stream_key, dims, scale, bound, cuts=(), held_as=jnp.bfloat16):
    result = jax.random.normal(stream_key, dims, jnp.float32) * scale
    if len(cuts) > 0:
        result = block_scale(stream_key, dims, cuts, -0.22, 0.18) * result
    return jnp.clip(result, min=-bound, max=bound).astype(held_as)


def setup_inputs(seed: int = 0, part: int = 0) -> dict:
    keys = jax.random.split(jax.random.key(seed), 5)
    own_keys = jax.random.split(jax.random.fold_in(keys[4], part), 5)
    height = bell_draw(own_keys[0], (NX, NY), 0.3, 2.5, ((0, 4), (1, 4)), jnp.float32)
    rigidity = jnp.clip(jnp.exp(math.log(1.6) - 1.3862944 * jax.random.uniform(own_keys[1], (NX, NY), jnp.float32) ** block_scale(own_keys[1], (NX, NY), ((0, 4), (1, 4)), -0.2, 0.2)), 0.4, 1.6)
    adhesion = jnp.clip(jnp.exp(math.log(10.0) - 2.3025851 * jax.random.uniform(own_keys[2], (NX, NY), jnp.float32) ** block_scale(own_keys[2], (NX, NY), ((0, 4), (1, 4)), -0.2, 0.2)), 1.0, 10.0)
    forcing = bell_draw(own_keys[3], (SUB, NX, NY), 1.0, 6.0, ((1, 4), (2, 4)))
    return dict(height=height, rigidity=rigidity, adhesion=adhesion, forcing=forcing)


step_size = 0.008
wave_floor = 0.25

def lap_four(grid):
    middle = grid[2:-2, 2:-2]
    first_dir = -grid[:-4, 2:-2] + 16.0 * grid[1:-3, 2:-2] - 30.0 * middle + 16.0 * grid[3:-1, 2:-2] - grid[4:, 2:-2]
    second_dir = -grid[2:-2, :-4] + 16.0 * grid[2:-2, 1:-3] - 30.0 * middle + 16.0 * grid[2:-2, 3:-1] - grid[2:-2, 4:]
    return (first_dir + second_dir) / 12.0

def slope_sq(grid):
    slope_rows = (grid[:-4, 2:-2] - 8.0 * grid[1:-3, 2:-2] + 8.0 * grid[3:-1, 2:-2] - grid[4:, 2:-2]) / 12.0
    slope_cols = (grid[2:-2, :-4] - 8.0 * grid[2:-2, 1:-3] + 8.0 * grid[2:-2, 3:-1] - grid[2:-2, 4:]) / 12.0
    return slope_rows * slope_rows + slope_cols * slope_cols

def substep(padded, rigidity, adhesion, noise_now):
    metric = 1.0 + slope_sq(padded)
    curvature = lap_four(padded) / (metric * jnp.sqrt(metric))
    bending = rigidity * lap_four(curvature)
    center = padded[4:-4, 4:-4]
    binding = adhesion * center * jnp.exp(-0.5 * center * center)
    return center + step_size * (noise_now - bending - binding)

def phase_table(row_start, extent, col_start, span_len, period):
    coarse_count = -(-extent // 64)
    col_ids = col_start + lax.iota(jnp.int32, span_len)[None, :]
    coarse_ids = row_start + 64 * lax.iota(jnp.int32, coarse_count)[:, None]
    fine_ids = lax.iota(jnp.int32, 64)[:, None]
    unit = 2.0 * math.pi / period
    coarse_angle = (coarse_ids * col_ids % period).astype(jnp.float32) * unit
    fine_angle = (fine_ids * col_ids % period).astype(jnp.float32) * unit
    cos_p = jnp.cos(coarse_angle)[:, None, :]
    sin_p = jnp.sin(coarse_angle)[:, None, :]
    cos_q = jnp.cos(fine_angle)[None, :, :]
    sin_q = jnp.sin(fine_angle)[None, :, :]
    cosines = (cos_p * cos_q - sin_p * sin_q).reshape(coarse_count * 64, span_len)[:extent]
    sines = (sin_p * cos_q + cos_p * sin_q).reshape(coarse_count * 64, span_len)[:extent]
    return (cosines.astype(jnp.bfloat16), sines.astype(jnp.bfloat16))

def reference(height, rigidity, adhesion, forcing):
    surface = height
    for iteration in range(SUB):
        padded = jnp.pad(surface, 4, mode='wrap')
        surface = substep(padded, rigidity, adhesion, forcing[iteration].astype(jnp.float32))
    velocity = ((surface - height) / (SUB * step_size)).astype(jnp.bfloat16)
    block_len = max(512, -(-KX // 8))
    real_list = []
    sine_list = []
    for offset in range(0, KX, block_len):
        extent = min(block_len, KX - offset)
        cos_x, sin_x = phase_table(offset, extent, 0, NX, NX)
        real_list.append(jnp.dot(cos_x, velocity, preferred_element_type=jnp.float32).astype(jnp.bfloat16))
        sine_list.append((-jnp.dot(sin_x, velocity, preferred_element_type=jnp.float32)).astype(jnp.bfloat16))
    real_x = jnp.concatenate(real_list, axis=0)
    sine_x = jnp.concatenate(sine_list, axis=0)
    wave_re_list = []
    wave_im_list = []
    for offset in range(0, NY, CC):
        cos_y, sin_y = phase_table(offset, CC, 0, NY, NY)
        wave_re_list.append(jnp.dot(cos_y, real_x.T, preferred_element_type=jnp.float32) + jnp.dot(sin_y, sine_x.T, preferred_element_type=jnp.float32))
        wave_im_list.append(jnp.dot(cos_y, sine_x.T, preferred_element_type=jnp.float32) - jnp.dot(sin_y, real_x.T, preferred_element_type=jnp.float32))
    wave_re = jnp.concatenate(wave_re_list, axis=0)
    wave_im = jnp.concatenate(wave_im_list, axis=0)
    wave_y = lax.iota(jnp.int32, NY)
    signed = jnp.where(wave_y < NY // 2, wave_y, wave_y - NY)
    angle_y = signed.astype(jnp.float32) * (2.0 * math.pi / NY)
    angle_x = lax.iota(jnp.int32, KX).astype(jnp.float32) * (2.0 * math.pi / NX)
    squared = angle_y[:, None] * angle_y[:, None] + angle_x[None, :] * angle_x[None, :]
    mobility = 1.0 / (2.0 * jnp.sqrt(squared + wave_floor)) / math.sqrt(NX * NY)
    spectrum = jnp.stack([wave_re * mobility, wave_im * mobility], axis=1)
    return (surface, spectrum)
```

```python
import functools
import math

import jax
import jax.numpy as jnp
from jax import lax
from jax.experimental import pallas as pl
from jax.experimental.pallas import tpu as pltpu
from jax.sharding import PartitionSpec as P

step_size = 0.008
wave_floor = 0.25

LANES = 128
HALO = 16
PAD = 16


def phase_rows(start, modes, period):
    ks = jnp.concatenate(
        [
            8 * lax.iota(jnp.int32, 8),
            lax.iota(jnp.int32, 8),
            start + 64 * lax.iota(jnp.int32, modes // 64),
        ]
    )
    angle = (ks[:, None] * lax.iota(jnp.int32, period)[None, :] % period).astype(jnp.float32) * (
        2.0 * math.pi / period
    )
    return jnp.cos(angle), jnp.sin(angle)


def write_table(cos_ref, sin_ref, width, store):
    rows, period = cos_ref.shape

    def columns(i, carry):
        lanes = pl.ds(pl.multiple_of(i * width, width), width)
        cos_c, sin_c = cos_ref[0:8, lanes], sin_ref[0:8, lanes]
        cos_b, sin_b = cos_ref[8:16, lanes], sin_ref[8:16, lanes]
        for a in range(rows - 16):
            cos_a, sin_a = cos_ref[16 + a : 17 + a, lanes], sin_ref[16 + a : 17 + a, lanes]
            cos_ac = cos_a * cos_c - sin_a * sin_c
            sin_ac = sin_a * cos_c + cos_a * sin_c
            for c in range(0, 8, 2):
                cosines, sines = [], []
                for d in (c, c + 1):
                    cos_r, sin_r = cos_ac[d : d + 1], sin_ac[d : d + 1]
                    cosines.append(cos_r * cos_b - sin_r * sin_b)
                    sines.append(sin_r * cos_b + cos_r * sin_b)
                store(i, 64 * a + 8 * c, jnp.concatenate(cosines, 0), jnp.concatenate(sines, 0))
        return carry

    lax.fori_loop(0, period // width, columns, 0)


def shifted(block, axis):
    size = block.shape[axis]
    return [pltpu.roll(block, shift % size, axis) for shift in (2, 1, -1, -2)]


def second_diff(block, rows, cols):
    ends = rows[0] + rows[3] + cols[0] + cols[3]
    near = rows[1] + rows[2] + cols[1] + cols[2]
    return (16.0 * near - ends - 60.0 * block) * (1.0 / 12.0)


def first_diff(moved):
    return ((moved[0] - moved[3]) + 8.0 * (moved[2] - moved[1])) * (1.0 / 12.0)


def kernel(
    substeps,
    n_row,
    n_col,
    height_ref,
    rigid_ref,
    adhes_ref,
    force_ref,
    cosx_ref,
    sinx_ref,
    cosy_ref,
    siny_ref,
    new_ref,
    wave_ref,
    surf,
    curv,
    extra,
    side_send,
    side_recv,
    edge_send,
    edge_recv,
    table_x,
    table_y,
    vel,
    modes,
    side_ssem,
    side_rsem,
    edge_ssem,
    edge_rsem,
    vel_ssem,
    vel_rsem,
    mode_ssem,
    mode_rsem,
):
    rows, cols = height_ref.shape
    chunks = cols // LANES
    wide = cols + LANES
    me_r = lax.axis_index("row")
    me_c = lax.axis_index("col")
    down = lax.rem(me_r + 1, n_row)
    up = lax.rem(me_r + n_row - 1, n_row)
    right = lax.rem(me_c + 1, n_col)
    left = lax.rem(me_c + n_col - 1, n_col)
    sibling = me_c + 1 - 2 * lax.rem(me_c, 2)
    mesh_ids = pl.DeviceIdType.MESH

    barrier = pltpu.get_barrier_semaphore()
    for target in (down, up):
        pl.semaphore_signal(barrier, inc=1, device_id={"row": target}, device_id_type=mesh_ids)
    for off in range(1, n_col):
        pl.semaphore_signal(
            barrier,
            inc=1,
            device_id={"col": lax.rem(me_c + off, n_col)},
            device_id_type=mesh_ids,
        )

    def send(src, dst, ssem, rsem, where):
        return pltpu.make_async_remote_copy(
            src_ref=src,
            dst_ref=dst,
            send_sem=ssem,
            recv_sem=rsem,
            device_id=where,
            device_id_type=mesh_ids,
        )

    pack_rows = 32

    def pack(i, carry):
        at = pl.ds(pl.multiple_of(i * pack_rows, pack_rows), pack_rows)
        slot = lax.broadcasted_iota(jnp.int32, (pack_rows, LANES), 1) // HALO
        for side in range(2):
            lanes = slice(0, LANES) if side == 0 else slice(cols - LANES, cols)
            base = 0 if side == 0 else HALO
            first = height_ref[at, lanes]
            coarse = first.astype(jnp.bfloat16).astype(jnp.float32)
            fields = [coarse, first - coarse, rigid_ref[at, lanes], adhes_ref[at, lanes]]
            for s in range(substeps):
                fields.append(force_ref[s, at, lanes].astype(jnp.float32))
            tile = jnp.zeros((pack_rows, LANES), jnp.float32)
            for f, field in enumerate(fields):
                turn = (f * HALO + base) % LANES
                moved = pltpu.roll(field, turn, 1) if turn else field
                tile = jnp.where(slot == f, moved, tile)
            side_send[side, at, :] = tile.astype(jnp.bfloat16)
        return carry

    lax.fori_loop(0, rows // pack_rows, pack, 0)
    pl.semaphore_wait(barrier, 2 + n_col - 1)

    sides = [
        send(side_send.at[k], side_recv.at[k], side_ssem.at[k], side_rsem.at[k], {"col": where})
        for k, where in ((0, left), (1, right))
    ]
    for copy in sides:
        copy.start()

    modes_here = table_x.shape[0] // 2

    def store_x(i, row, cosines, sines):
        lanes = pl.ds(pl.multiple_of(i * cols, cols), cols)
        table_x[row : row + 16, lanes] = cosines.astype(jnp.bfloat16)
        table_x[modes_here + row : modes_here + row + 16, lanes] = (-sines).astype(jnp.bfloat16)

    write_table(cosx_ref, sinx_ref, cols, store_x)

    for copy in sides:
        copy.wait_recv()

    def unpack(i, carry):
        at = pl.ds(pl.multiple_of(i * pack_rows, pack_rows), pack_rows)
        lane = lax.broadcasted_iota(jnp.int32, (pack_rows, LANES), 1)
        after = side_recv[0, at, :].astype(jnp.float32)
        before = side_recv[1, at, :].astype(jnp.float32)
        got = []
        for f in range(4 + substeps):
            turn_a = (-f * HALO) % LANES
            turn_b = (-HALO - f * HALO) % LANES
            a = pltpu.roll(after, turn_a, 1) if turn_a else after
            b = pltpu.roll(before, turn_b, 1) if turn_b else before
            got.append(jnp.where(lane < LANES // 2, a, b))
        inside = pl.ds(pl.multiple_of(i * pack_rows + PAD, 16), pack_rows)
        surf[inside, 0:cols] = height_ref[at, :]
        surf[inside, cols:wide] = got[0] + got[1]
        for f in range(2, 4 + substeps):
            extra[f - 2, at, :] = got[f]
        return carry

    lax.fori_loop(0, rows // pack_rows, unpack, 0)

    def edge_copies(s):
        return [
            send(
                edge_send.at[s, k],
                edge_recv.at[s, k],
                edge_ssem.at[s, k],
                edge_rsem.at[s, k],
                {"row": where},
            )
            for k, where in ((0, up), (1, down))
        ]

    def send_edges(s):
        edge_send[s, 0] = surf[PAD : PAD + 8, :]
        edge_send[s, 1] = surf[PAD + rows - 8 : PAD + rows, :]
        copies = edge_copies(s)
        for copy in copies:
            copy.start()
        return copies

    def bend(start, count):
        block = surf[pl.ds(start - 8, count + 16), :]
        moved_rows = [m[8:-8] for m in shifted(block, 0)]
        middle = block[8:-8]
        moved_cols = shifted(middle, 1)
        slope_r = first_diff(moved_rows)
        slope_c = first_diff(moved_cols)
        metric = 1.0 + (slope_r * slope_r + slope_c * slope_c)
        inverse = lax.rsqrt(metric)
        curv[pl.ds(start, count), :] = (
            second_diff(middle, moved_rows, moved_cols) * (inverse * inverse * inverse)
        )

    def advance(start, count, s):
        inside = pl.ds(start + PAD, count)
        at = pl.ds(start, count)
        block = curv[pl.ds(start + PAD - 8, count + 16), :]
        moved_rows = [m[8:-8] for m in shifted(block, 0)]
        middle = block[8:-8]
        lap = second_diff(middle, moved_rows, shifted(middle, 1))
        rigid = jnp.concatenate([rigid_ref[at, :], extra[0, at, :]], 1)
        adhes = jnp.concatenate([adhes_ref[at, :], extra[1, at, :]], 1)
        noise = jnp.concatenate([force_ref[s, at, :].astype(jnp.float32), extra[2 + s, at, :]], 1)
        center = surf[inside, :]
        binding = adhes * center * jnp.exp(-0.5 * center * center)
        result = center + step_size * (noise - rigid * lap - binding)
        if s < substeps - 1:
            surf[inside, :] = result
        else:
            final = result[:, 0:cols]
            new_ref[at, :] = final
            speed = ((final - height_ref[at, :]) * (1.0 / (substeps * step_size))).astype(
                jnp.bfloat16
            )
            for q in range(chunks):
                vel[q, pl.ds(pl.multiple_of(me_r * rows, rows) + start, count), :] = speed[
                    :, q * LANES : (q + 1) * LANES
                ]

    inner = rows - 32
    strip = next(k for k in (48, 32, 16) if inner % k == 0)

    pending = send_edges(0)
    edges = list(pending)
    for s in range(substeps):

        def bend_strip(i, carry):
            bend(pl.multiple_of(PAD + 16 + i * strip, 16), strip)
            return carry

        def advance_strip(i, carry, s=s):
            advance(pl.multiple_of(16 + i * strip, 16), strip, s)
            return carry

        lax.fori_loop(0, inner // strip, bend_strip, 0)
        for copy in pending:
            copy.wait_recv()
        surf[PAD - 8 : PAD, :] = edge_recv[s, 1]
        surf[PAD + rows : PAD + rows + 8, :] = edge_recv[s, 0]
        bend(PAD - 8, 24)
        bend(PAD + rows - 16, 24)
        advance(0, 16, s)
        advance(rows - 16, 16, s)
        if s < substeps - 1:
            pending = send_edges(s + 1)
            edges += pending
        lax.fori_loop(0, inner // strip, advance_strip, 0)

    def vel_copy(way, distance, q):
        owner = me_r - distance if way == 0 else me_r + distance
        where = down if way == 0 else up
        part = vel.at[q, pl.ds(pl.multiple_of(owner * rows, rows), rows), :]
        sems = (way, distance, q)
        return send(part, part, vel_ssem.at[sems], vel_rsem.at[sems], {"row": where})

    def can_send(way, distance):
        if way == 0:
            return jnp.logical_and(me_r >= distance, me_r + 1 < n_row)
        return jnp.logical_and(me_r + distance < n_row, me_r > 0)

    def has_block(way, distance):
        return me_r >= distance if way == 0 else me_r + distance < n_row

    def vel_arrival(way, distance, q):
        owner = me_r - distance if way == 0 else me_r + distance
        part = vel.at[q, pl.ds(pl.multiple_of(owner * rows, rows), rows), :]
        sems = (way, distance - 1, q)
        where = down if way == 0 else up
        return send(part, part, vel_ssem.at[sems], vel_rsem.at[sems], {"row": where})

    def push(way, distance, q):
        @pl.when(can_send(way, distance))
        def _():
            vel_copy(way, distance, q).start()

    for q in range(chunks):
        for way in range(2):
            push(way, 0, q)

    def store_y(i, row, cosines, sines):
        lanes = pl.ds(pl.multiple_of(i * LANES, LANES), LANES)
        for q in range(chunks):
            part = slice(q * LANES, (q + 1) * LANES)
            table_y[q, row : row + 16, lanes] = cosines[:, part].astype(jnp.bfloat16)
            table_y[q, cols + row : cols + row + 16, lanes] = sines[:, part].astype(jnp.bfloat16)

    write_table(cosy_ref, siny_ref, cols, store_y)

    def mode_part(q, owner):
        return modes.at[q, :, pl.ds(pl.multiple_of(owner * LANES, LANES), LANES)]

    def mode_copy(q, owner, slot, where):
        part = mode_part(q, owner)
        return send(part, part, mode_ssem.at[q, slot], mode_rsem.at[q, slot], {"col": where})

    pairs = n_col // 2
    for q in range(chunks):
        for distance in range(1, n_row):
            for way in range(2):

                @pl.when(has_block(way, distance))
                def _(way=way, distance=distance, q=q):
                    vel_arrival(way, distance, q).wait_recv()

                if distance < n_row - 1:
                    push(way, distance, q)
        result = jnp.dot(table_x[...], vel[q], preferred_element_type=jnp.float32)
        mine = pl.ds(pl.multiple_of(me_c * LANES, LANES), LANES)
        modes[q, :, mine] = result.astype(jnp.bfloat16)
        for off in range(1, pairs):
            mode_copy(q, me_c, pairs - 1 + off, lax.rem(me_c + 2 * off, n_col)).start()
        mode_copy(q, me_c, 0, sibling).start()

    for q in range(chunks):
        for off in range(1, pairs):
            owner = lax.rem(me_c + n_col - 2 * off, n_col)
            mode_copy(q, owner, pairs - 1 + off, sibling).wait_recv()
            mode_copy(q, owner, off, sibling).start()
        mode_copy(q, sibling, 0, sibling).wait_recv()
        for off in range(1, pairs):
            owner = lax.rem(sibling + n_col - 2 * off, n_col)
            mode_copy(q, owner, off, sibling).wait_recv()
        terms = lax.dot_general(
            table_y[q], modes[q], (((1,), (1,)), ((), ())), preferred_element_type=jnp.float32
        )
        k = modes_here
        real = terms[:cols, :k] + terms[cols:, k:]
        imag = terms[:cols, k:] - terms[cols:, :k]
        if q == 0:
            wave_ref[:, :k] = real
            wave_ref[:, k:] = imag
        else:
            wave_ref[:, :k] += real
            wave_ref[:, k:] += imag

    for copy in sides + edges:
        copy.wait_send()
    for q in range(chunks):
        for distance in range(n_row - 1):
            for way in range(2):

                @pl.when(can_send(way, distance))
                def _(way=way, distance=distance, q=q):
                    vel_copy(way, distance, q).wait_send()

        for off in range(1, pairs):
            mode_copy(q, me_c, pairs - 1 + off, lax.rem(me_c + 2 * off, n_col)).wait_send()
            mode_copy(q, me_c, off, sibling).wait_send()
        mode_copy(q, me_c, 0, sibling).wait_send()


def on_device(height, rigidity, adhesion, forcing):
    rows, cols = height.shape
    substeps = forcing.shape[0]
    n_row = lax.axis_size("row")
    n_col = lax.axis_size("col")
    full_rows, full_cols = rows * n_row, cols * n_col
    local_modes = full_rows // 2 // n_row
    chunks = cols // LANES
    pairs = n_col // 2
    wide = cols + LANES
    row_at = lax.axis_index("row") * local_modes
    col_at = lax.axis_index("col") * cols
    cos_x, sin_x = phase_rows(row_at, local_modes, full_rows)
    cos_y, sin_y = phase_rows(col_at, cols, full_cols)
    f32, bf16 = jnp.float32, jnp.bfloat16
    dma = pltpu.SemaphoreType.DMA
    vmem = pl.BlockSpec(memory_space=pltpu.VMEM)
    new_height, waves = pl.pallas_call(
        functools.partial(kernel, substeps, n_row, n_col),
        out_shape=(
            jax.ShapeDtypeStruct((rows, cols), f32),
            jax.ShapeDtypeStruct((cols, 2 * local_modes), f32),
        ),
        in_specs=[vmem] * 8,
        out_specs=(vmem, vmem),
        scratch_shapes=[
            pltpu.VMEM((rows + 2 * PAD, wide), f32),
            pltpu.VMEM((rows + 2 * PAD, wide), f32),
            pltpu.VMEM((2 + substeps, rows, LANES), f32),
            pltpu.VMEM((2, rows, LANES), bf16),
            pltpu.VMEM((2, rows, LANES), bf16),
            pltpu.VMEM((substeps, 2, 8, wide), f32),
            pltpu.VMEM((substeps, 2, 8, wide), f32),
            pltpu.VMEM((2 * local_modes, full_rows), bf16),
            pltpu.VMEM((chunks, 2 * cols, n_col * LANES), bf16),
            pltpu.VMEM((chunks, full_rows, LANES), bf16),
            pltpu.VMEM((chunks, 2 * local_modes, n_col * LANES), bf16),
            dma((2,)),
            dma((2,)),
            dma((substeps, 2)),
            dma((substeps, 2)),
            dma((2, n_row - 1, chunks)),
            dma((2, n_row - 1, chunks)),
            dma((chunks, 2 * pairs - 1)),
            dma((chunks, 2 * pairs - 1)),
        ],
        compiler_params=pltpu.CompilerParams(
            collective_id=0, has_side_effects=True, vmem_limit_bytes=48 * 1024 * 1024
        ),
    )(height, rigidity, adhesion, forcing, cos_x, sin_x, cos_y, sin_y)
    wave_y = col_at + lax.iota(jnp.int32, cols)
    signed = jnp.where(wave_y < full_cols // 2, wave_y, wave_y - full_cols)
    angle_y = signed.astype(f32) * (2.0 * math.pi / full_cols)
    wave_x = row_at + lax.iota(jnp.int32, local_modes)
    angle_x = wave_x.astype(f32) * (2.0 * math.pi / full_rows)
    squared = angle_y[:, None] * angle_y[:, None] + angle_x[None, :] * angle_x[None, :]
    mobility = 1.0 / (2.0 * jnp.sqrt(squared + wave_floor)) / math.sqrt(full_rows * full_cols)
    spectrum = waves.reshape(cols, 2, local_modes) * mobility[:, None, :]
    return (new_height, spectrum)


def solution(mesh):
    in_specs = (
        P(("groups", "row"), "col"),
        P(("groups", "row"), "col"),
        P(("groups", "row"), "col"),
        P(None, ("groups", "row"), "col"),
    )
    out_specs = (P(("groups", "row"), "col"), P(("groups", "col"), None, "row"))
    return jax.shard_map(
        on_device, mesh=mesh, in_specs=in_specs, out_specs=out_specs, check_vma=False
    )
```

```python
import functools
import math

import jax
import jax.numpy as jnp
from jax import lax
from jax.experimental import pallas as pl
from jax.experimental.pallas import tpu as pltpu
from jax.sharding import PartitionSpec as P

step_size = 0.008
wave_floor = 0.25

LANES = 128
HALO = 16
PAD = 16


def write_phases(start, cos_ref, sin_ref):
    rows, period = cos_ref.shape
    width = 2 * LANES

    def columns(i, carry):
        at = pl.multiple_of(i * width, width)
        for top in range(0, rows, 8):
            k = lax.broadcasted_iota(jnp.int32, (8, width), 0)
            if top == 0:
                k = 8 * k
            elif top >= 16:
                k = start + 64 * (top - 16 + k)
            turn = lax.rem(k * (at + lax.broadcasted_iota(jnp.int32, (8, width), 1)), period)
            quarter = jnp.zeros_like(turn)
            for edge in (1, 3, 5, 7):
                quarter += (turn >= edge * period // 8).astype(jnp.int32)
            x = (turn - quarter * (period // 4)).astype(jnp.float32) * (2.0 * math.pi / period)
            y = x * x
            sine = x * (1.0 + y * (-1 / 6 + y * (1 / 120 + y * (-1 / 5040 + y * (1 / 362880)))))
            cosine = 1.0 + y * (-1 / 2 + y * (1 / 24 + y * (-1 / 720 + y * (1 / 40320))))
            odd = jnp.logical_or(quarter == 1, quarter == 3)
            first = jnp.where(odd, sine, cosine)
            second = jnp.where(odd, cosine, sine)
            minus_cos = jnp.logical_or(quarter == 1, quarter == 2)
            minus_sin = jnp.logical_or(quarter == 2, quarter == 3)
            cos_ref[top : top + 8, pl.ds(at, width)] = jnp.where(minus_cos, -first, first)
            sin_ref[top : top + 8, pl.ds(at, width)] = jnp.where(minus_sin, -second, second)
        return carry

    lax.fori_loop(0, period // width, columns, 0)


def write_table(cos_ref, sin_ref, coarse, width, store):
    period = cos_ref.shape[1]

    def columns(i, carry):
        lanes = pl.ds(pl.multiple_of(i * width, width), width)
        cos_c, sin_c = cos_ref[0:8, lanes], sin_ref[0:8, lanes]
        cos_b, sin_b = cos_ref[8:16, lanes], sin_ref[8:16, lanes]
        for a in range(coarse):
            cos_a, sin_a = cos_ref[16 + a : 17 + a, lanes], sin_ref[16 + a : 17 + a, lanes]
            cos_ac = cos_a * cos_c - sin_a * sin_c
            sin_ac = sin_a * cos_c + cos_a * sin_c
            for c in range(0, 8, 2):
                cosines, sines = [], []
                for d in (c, c + 1):
                    cos_r, sin_r = cos_ac[d : d + 1], sin_ac[d : d + 1]
                    cosines.append(cos_r * cos_b - sin_r * sin_b)
                    sines.append(sin_r * cos_b + cos_r * sin_b)
                store(i, 64 * a + 8 * c, jnp.concatenate(cosines, 0), jnp.concatenate(sines, 0))
        return carry

    lax.fori_loop(0, period // width, columns, 0)


def shifted(block, axis):
    size = block.shape[axis]
    return [pltpu.roll(block, shift % size, axis) for shift in (2, 1, -1, -2)]


def second_diff(block, rows, cols):
    ends = rows[0] + rows[3] + cols[0] + cols[3]
    near = rows[1] + rows[2] + cols[1] + cols[2]
    return (16.0 * near - ends - 60.0 * block) * (1.0 / 12.0)


def first_diff(moved):
    return ((moved[0] - moved[3]) + 8.0 * (moved[2] - moved[1])) * (1.0 / 12.0)


def kernel(
    substeps,
    n_row,
    n_col,
    height_in,
    rigid_in,
    adhes_in,
    force_in,
    new_out,
    wave_ref,
    height_ref,
    rigid_ref,
    adhes_ref,
    force_ref,
    new_ref,
    cosx_ref,
    sinx_ref,
    cosy_ref,
    siny_ref,
    surf,
    curv,
    extra,
    side_send,
    side_recv,
    edge_send,
    edge_recv,
    table_x,
    table_y,
    vel,
    modes,
    side_ssem,
    side_rsem,
    edge_ssem,
    edge_rsem,
    vel_ssem,
    vel_rsem,
    mode_ssem,
    mode_rsem,
    load_sem,
    out_sem,
):
    rows, cols = height_ref.shape
    chunks = cols // LANES
    wide = cols + LANES
    me_r = lax.axis_index("row")
    me_c = lax.axis_index("col")
    down = lax.rem(me_r + 1, n_row)
    up = lax.rem(me_r + n_row - 1, n_row)
    right = lax.rem(me_c + 1, n_col)
    left = lax.rem(me_c + n_col - 1, n_col)
    sibling = me_c + 1 - 2 * lax.rem(me_c, 2)
    mesh_ids = pl.DeviceIdType.MESH

    loads = [
        pltpu.make_async_copy(src, dst, load_sem.at[i])
        for i, (src, dst) in enumerate(
            (
                (height_in, height_ref),
                (rigid_in, rigid_ref),
                (adhes_in, adhes_ref),
                (force_in, force_ref),
            )
        )
    ]
    for copy in loads:
        copy.start()

    barrier = pltpu.get_barrier_semaphore()
    for target in (down, up):
        pl.semaphore_signal(barrier, inc=1, device_id={"row": target}, device_id_type=mesh_ids)
    for off in range(1, n_col):
        pl.semaphore_signal(
            barrier,
            inc=1,
            device_id={"col": lax.rem(me_c + off, n_col)},
            device_id_type=mesh_ids,
        )

    def send(src, dst, ssem, rsem, where):
        return pltpu.make_async_remote_copy(
            src_ref=src,
            dst_ref=dst,
            send_sem=ssem,
            recv_sem=rsem,
            device_id=where,
            device_id_type=mesh_ids,
        )

    pack_rows = 32
    for copy in loads:
        copy.wait()

    def pack(i, carry):
        at = pl.ds(pl.multiple_of(i * pack_rows, pack_rows), pack_rows)
        slot = lax.broadcasted_iota(jnp.int32, (pack_rows, LANES), 1) // HALO
        for side in range(2):
            lanes = slice(0, LANES) if side == 0 else slice(cols - LANES, cols)
            base = 0 if side == 0 else HALO
            first = height_ref[at, lanes]
            coarse = first.astype(jnp.bfloat16).astype(jnp.float32)
            fields = [coarse, first - coarse, rigid_ref[at, lanes], adhes_ref[at, lanes]]
            for s in range(substeps):
                fields.append(force_ref[s, at, lanes].astype(jnp.float32))
            tile = jnp.zeros((pack_rows, LANES), jnp.float32)
            for f, field in enumerate(fields):
                turn = (f * HALO + base) % LANES
                moved = pltpu.roll(field, turn, 1) if turn else field
                tile = jnp.where(slot == f, moved, tile)
            side_send[side, at, :] = tile.astype(jnp.bfloat16)
        return carry

    lax.fori_loop(0, rows // pack_rows, pack, 0)
    pl.semaphore_wait(barrier, 2 + n_col - 1)

    sides = [
        send(side_send.at[k], side_recv.at[k], side_ssem.at[k], side_rsem.at[k], {"col": where})
        for k, where in ((0, left), (1, right))
    ]
    for copy in sides:
        copy.start()

    modes_here = table_x.shape[0] // 2

    def store_x(i, row, cosines, sines):
        lanes = pl.ds(pl.multiple_of(i * cols, cols), cols)
        table_x[row : row + 16, lanes] = cosines.astype(jnp.bfloat16)
        table_x[modes_here + row : modes_here + row + 16, lanes] = (-sines).astype(jnp.bfloat16)

    write_phases(me_r * modes_here, cosx_ref, sinx_ref)
    write_table(cosx_ref, sinx_ref, modes_here // 64, cols, store_x)

    for copy in sides:
        copy.wait_recv()

    def unpack(i, carry):
        at = pl.ds(pl.multiple_of(i * pack_rows, pack_rows), pack_rows)
        lane = lax.broadcasted_iota(jnp.int32, (pack_rows, LANES), 1)
        after = side_recv[0, at, :].astype(jnp.float32)
        before = side_recv[1, at, :].astype(jnp.float32)
        got = []
        for f in range(4 + substeps):
            turn_a = (-f * HALO) % LANES
            turn_b = (-HALO - f * HALO) % LANES
            a = pltpu.roll(after, turn_a, 1) if turn_a else after
            b = pltpu.roll(before, turn_b, 1) if turn_b else before
            got.append(jnp.where(lane < LANES // 2, a, b))
        inside = pl.ds(pl.multiple_of(i * pack_rows + PAD, 16), pack_rows)
        surf[inside, 0:cols] = height_ref[at, :]
        surf[inside, cols:wide] = got[0] + got[1]
        for f in range(2, 4 + substeps):
            extra[f - 2, at, :] = got[f]
        return carry

    lax.fori_loop(0, rows // pack_rows, unpack, 0)

    def edge_copies(s):
        return [
            send(
                edge_send.at[s, k],
                edge_recv.at[s, k],
                edge_ssem.at[s, k],
                edge_rsem.at[s, k],
                {"row": where},
            )
            for k, where in ((0, up), (1, down))
        ]

    def send_edges(s):
        edge_send[s, 0] = surf[PAD : PAD + 8, :]
        edge_send[s, 1] = surf[PAD + rows - 8 : PAD + rows, :]
        copies = edge_copies(s)
        for copy in copies:
            copy.start()
        return copies

    def bend(start, count):
        block = surf[pl.ds(start - 8, count + 16), :]
        moved_rows = [m[8:-8] for m in shifted(block, 0)]
        middle = block[8:-8]
        moved_cols = shifted(middle, 1)
        slope_r = first_diff(moved_rows)
        slope_c = first_diff(moved_cols)
        metric = 1.0 + (slope_r * slope_r + slope_c * slope_c)
        inverse = lax.rsqrt(metric)
        curv[pl.ds(start, count), :] = (
            second_diff(middle, moved_rows, moved_cols) * (inverse * inverse * inverse)
        )

    def advance(start, count, s):
        inside = pl.ds(start + PAD, count)
        at = pl.ds(start, count)
        block = curv[pl.ds(start + PAD - 8, count + 16), :]
        moved_rows = [m[8:-8] for m in shifted(block, 0)]
        middle = block[8:-8]
        lap = second_diff(middle, moved_rows, shifted(middle, 1))
        rigid = jnp.concatenate([rigid_ref[at, :], extra[0, at, :]], 1)
        adhes = jnp.concatenate([adhes_ref[at, :], extra[1, at, :]], 1)
        noise = jnp.concatenate([force_ref[s, at, :].astype(jnp.float32), extra[2 + s, at, :]], 1)
        center = surf[inside, :]
        binding = adhes * center * jnp.exp(-0.5 * center * center)
        result = center + step_size * (noise - rigid * lap - binding)
        if s < substeps - 1:
            surf[inside, :] = result
        else:
            final = result[:, 0:cols]
            new_ref[at, :] = final
            speed = ((final - height_ref[at, :]) * (1.0 / (substeps * step_size))).astype(
                jnp.bfloat16
            )
            for q in range(chunks):
                vel[q, pl.ds(pl.multiple_of(me_r * rows, rows) + start, count), :] = speed[
                    :, q * LANES : (q + 1) * LANES
                ]

    inner = rows - 32
    strip = next(k for k in (96, 48, 32, 16) if inner % k == 0)

    pending = send_edges(0)
    edges = list(pending)
    for s in range(substeps):

        def bend_strip(i, carry):
            bend(pl.multiple_of(PAD + 16 + i * strip, 16), strip)
            return carry

        def advance_strip(i, carry, s=s):
            advance(pl.multiple_of(16 + i * strip, 16), strip, s)
            return carry

        lax.fori_loop(0, inner // strip, bend_strip, 0)
        for copy in pending:
            copy.wait_recv()
        surf[PAD - 8 : PAD, :] = edge_recv[s, 1]
        surf[PAD + rows : PAD + rows + 8, :] = edge_recv[s, 0]
        bend(PAD - 8, 24)
        bend(PAD + rows - 16, 24)
        advance(0, 16, s)
        advance(rows - 16, 16, s)
        if s < substeps - 1:
            pending = send_edges(s + 1)
            edges += pending
        lax.fori_loop(0, inner // strip, advance_strip, 0)

    def vel_copy(way, distance, q):
        owner = me_r - distance if way == 0 else me_r + distance
        where = down if way == 0 else up
        part = vel.at[q, pl.ds(pl.multiple_of(owner * rows, rows), rows), :]
        sems = (way, distance, q)
        return send(part, part, vel_ssem.at[sems], vel_rsem.at[sems], {"row": where})

    def can_send(way, distance):
        if way == 0:
            return jnp.logical_and(me_r >= distance, me_r + 1 < n_row)
        return jnp.logical_and(me_r + distance < n_row, me_r > 0)

    def has_block(way, distance):
        return me_r >= distance if way == 0 else me_r + distance < n_row

    def vel_arrival(way, distance, q):
        owner = me_r - distance if way == 0 else me_r + distance
        part = vel.at[q, pl.ds(pl.multiple_of(owner * rows, rows), rows), :]
        sems = (way, distance - 1, q)
        where = down if way == 0 else up
        return send(part, part, vel_ssem.at[sems], vel_rsem.at[sems], {"row": where})

    def push(way, distance, q):
        @pl.when(can_send(way, distance))
        def _():
            vel_copy(way, distance, q).start()

    for q in range(chunks):
        for way in range(2):
            push(way, 0, q)
    result_out = pltpu.make_async_copy(new_ref, new_out, out_sem)
    result_out.start()

    def store_y(i, row, cosines, sines):
        lanes = pl.ds(pl.multiple_of(i * LANES, LANES), LANES)
        for q in range(chunks):
            part = slice(q * LANES, (q + 1) * LANES)
            table_y[q, row : row + 16, lanes] = cosines[:, part].astype(jnp.bfloat16)
            table_y[q, cols + row : cols + row + 16, lanes] = sines[:, part].astype(jnp.bfloat16)

    write_phases(me_c * cols, cosy_ref, siny_ref)
    write_table(cosy_ref, siny_ref, cols // 64, cols, store_y)

    def mode_part(q, owner):
        return modes.at[q, :, pl.ds(pl.multiple_of(owner * LANES, LANES), LANES)]

    def mode_copy(q, owner, slot, where):
        part = mode_part(q, owner)
        return send(part, part, mode_ssem.at[q, slot], mode_rsem.at[q, slot], {"col": where})

    pairs = n_col // 2
    for q in range(chunks):
        for distance in range(1, n_row):
            for way in range(2):

                @pl.when(has_block(way, distance))
                def _(way=way, distance=distance, q=q):
                    vel_arrival(way, distance, q).wait_recv()

                if distance < n_row - 1:
                    push(way, distance, q)
        result = jnp.dot(table_x[...], vel[q], preferred_element_type=jnp.float32)
        mine = pl.ds(pl.multiple_of(me_c * LANES, LANES), LANES)
        modes[q, :, mine] = result.astype(jnp.bfloat16)
        for off in range(1, pairs):
            mode_copy(q, me_c, pairs - 1 + off, lax.rem(me_c + 2 * off, n_col)).start()
        mode_copy(q, me_c, 0, sibling).start()

    for q in range(chunks):
        for off in range(1, pairs):
            owner = lax.rem(me_c + n_col - 2 * off, n_col)
            mode_copy(q, owner, pairs - 1 + off, sibling).wait_recv()
            mode_copy(q, owner, off, sibling).start()
        mode_copy(q, sibling, 0, sibling).wait_recv()
        for off in range(1, pairs):
            owner = lax.rem(sibling + n_col - 2 * off, n_col)
            mode_copy(q, owner, off, sibling).wait_recv()
        terms = lax.dot_general(
            table_y[q], modes[q], (((1,), (1,)), ((), ())), preferred_element_type=jnp.float32
        )
        k = modes_here
        real = terms[:cols, :k] + terms[cols:, k:]
        imag = terms[:cols, k:] - terms[cols:, :k]
        if q == 0:
            wave_ref[:, :k] = real
            wave_ref[:, k:] = imag
        else:
            wave_ref[:, :k] += real
            wave_ref[:, k:] += imag

    result_out.wait()
    for copy in sides + edges:
        copy.wait_send()
    for q in range(chunks):
        for distance in range(n_row - 1):
            for way in range(2):

                @pl.when(can_send(way, distance))
                def _(way=way, distance=distance, q=q):
                    vel_copy(way, distance, q).wait_send()

        for off in range(1, pairs):
            mode_copy(q, me_c, pairs - 1 + off, lax.rem(me_c + 2 * off, n_col)).wait_send()
            mode_copy(q, me_c, off, sibling).wait_send()
        mode_copy(q, me_c, 0, sibling).wait_send()


def on_device(height, rigidity, adhesion, forcing):
    rows, cols = height.shape
    substeps = forcing.shape[0]
    n_row = lax.axis_size("row")
    n_col = lax.axis_size("col")
    full_rows, full_cols = rows * n_row, cols * n_col
    local_modes = full_rows // 2 // n_row
    chunks = cols // LANES
    pairs = n_col // 2
    wide = cols + LANES
    row_at = lax.axis_index("row") * local_modes
    col_at = lax.axis_index("col") * cols
    rows_x = 16 + -(-local_modes // 512) * 8
    rows_y = 16 + -(-cols // 512) * 8
    f32, bf16 = jnp.float32, jnp.bfloat16
    dma = pltpu.SemaphoreType.DMA
    hbm = pl.BlockSpec(memory_space=pltpu.HBM)
    vmem = pl.BlockSpec(memory_space=pltpu.VMEM)
    new_height, waves = pl.pallas_call(
        functools.partial(kernel, substeps, n_row, n_col),
        out_shape=(
            jax.ShapeDtypeStruct((rows, cols), f32),
            jax.ShapeDtypeStruct((cols, 2 * local_modes), f32),
        ),
        in_specs=[hbm] * 4,
        out_specs=(hbm, vmem),
        scratch_shapes=[
            pltpu.VMEM((rows, cols), f32),
            pltpu.VMEM((rows, cols), f32),
            pltpu.VMEM((rows, cols), f32),
            pltpu.VMEM((substeps, rows, cols), bf16),
            pltpu.VMEM((rows, cols), f32),
            pltpu.VMEM((rows_x, full_rows), f32),
            pltpu.VMEM((rows_x, full_rows), f32),
            pltpu.VMEM((rows_y, full_cols), f32),
            pltpu.VMEM((rows_y, full_cols), f32),
            pltpu.VMEM((rows + 2 * PAD, wide), f32),
            pltpu.VMEM((rows + 2 * PAD, wide), f32),
            pltpu.VMEM((2 + substeps, rows, LANES), f32),
            pltpu.VMEM((2, rows, LANES), bf16),
            pltpu.VMEM((2, rows, LANES), bf16),
            pltpu.VMEM((substeps, 2, 8, wide), f32),
            pltpu.VMEM((substeps, 2, 8, wide), f32),
            pltpu.VMEM((2 * local_modes, full_rows), bf16),
            pltpu.VMEM((chunks, 2 * cols, n_col * LANES), bf16),
            pltpu.VMEM((chunks, full_rows, LANES), bf16),
            pltpu.VMEM((chunks, 2 * local_modes, n_col * LANES), bf16),
            dma((2,)),
            dma((2,)),
            dma((substeps, 2)),
            dma((substeps, 2)),
            dma((2, n_row - 1, chunks)),
            dma((2, n_row - 1, chunks)),
            dma((chunks, 2 * pairs - 1)),
            dma((chunks, 2 * pairs - 1)),
            dma((4,)),
            dma,
        ],
        compiler_params=pltpu.CompilerParams(
            collective_id=0, has_side_effects=True, vmem_limit_bytes=127 * 512 * 1024
        ),
    )(height, rigidity, adhesion, forcing)
    wave_y = col_at + lax.iota(jnp.int32, cols)
    signed = jnp.where(wave_y < full_cols // 2, wave_y, wave_y - full_cols)
    angle_y = signed.astype(f32) * (2.0 * math.pi / full_cols)
    wave_x = row_at + lax.iota(jnp.int32, local_modes)
    angle_x = wave_x.astype(f32) * (2.0 * math.pi / full_rows)
    squared = angle_y[:, None] * angle_y[:, None] + angle_x[None, :] * angle_x[None, :]
    mobility = 1.0 / (2.0 * jnp.sqrt(squared + wave_floor)) / math.sqrt(full_rows * full_cols)
    spectrum = waves.reshape(cols, 2, local_modes) * mobility[:, None, :]
    return (new_height, spectrum)


def solution(mesh):
    in_specs = (
        P(("groups", "row"), "col"),
        P(("groups", "row"), "col"),
        P(("groups", "row"), "col"),
        P(None, ("groups", "row"), "col"),
    )
    out_specs = (P(("groups", "row"), "col"), P(("groups", "col"), None, "row"))
    return jax.shard_map(
        on_device, mesh=mesh, in_specs=in_specs, out_specs=out_specs, check_vma=False
    )
```

```python
import functools
import math

import jax
import jax.numpy as jnp
from jax import lax
from jax.experimental import pallas as pl
from jax.experimental.pallas import tpu as pltpu
from jax.sharding import PartitionSpec as P

step_size = 0.008
wave_floor = 0.25

LANES = 128
HALO = 16
PAD = 16


def write_phases(start, cos_ref, sin_ref):
    rows, period = cos_ref.shape
    width = 2 * LANES

    def columns(i, carry):
        at = pl.multiple_of(i * width, width)
        for top in range(0, rows, 8):
            k = lax.broadcasted_iota(jnp.int32, (8, width), 0)
            if top == 0:
                k = 8 * k
            elif top >= 16:
                k = start + 64 * (top - 16 + k)
            turn = lax.rem(k * (at + lax.broadcasted_iota(jnp.int32, (8, width), 1)), period)
            quarter = jnp.zeros_like(turn)
            for edge in (1, 3, 5, 7):
                quarter += (turn >= edge * period // 8).astype(jnp.int32)
            x = (turn - quarter * (period // 4)).astype(jnp.float32) * (2.0 * math.pi / period)
            y = x * x
            sine = x * (1.0 + y * (-1 / 6 + y * (1 / 120 + y * (-1 / 5040 + y * (1 / 362880)))))
            cosine = 1.0 + y * (-1 / 2 + y * (1 / 24 + y * (-1 / 720 + y * (1 / 40320))))
            odd = jnp.logical_or(quarter == 1, quarter == 3)
            first = jnp.where(odd, sine, cosine)
            second = jnp.where(odd, cosine, sine)
            minus_cos = jnp.logical_or(quarter == 1, quarter == 2)
            minus_sin = jnp.logical_or(quarter == 2, quarter == 3)
            cos_ref[top : top + 8, pl.ds(at, width)] = jnp.where(minus_cos, -first, first)
            sin_ref[top : top + 8, pl.ds(at, width)] = jnp.where(minus_sin, -second, second)
        return carry

    lax.fori_loop(0, period // width, columns, 0)


def write_table(cos_ref, sin_ref, coarse, width, store):
    period = cos_ref.shape[1]

    def columns(i, carry):
        lanes = pl.ds(pl.multiple_of(i * width, width), width)
        cos_c, sin_c = cos_ref[0:8, lanes], sin_ref[0:8, lanes]
        cos_b, sin_b = cos_ref[8:16, lanes], sin_ref[8:16, lanes]
        for a in range(coarse):
            cos_a, sin_a = cos_ref[16 + a : 17 + a, lanes], sin_ref[16 + a : 17 + a, lanes]
            cos_ac = cos_a * cos_c - sin_a * sin_c
            sin_ac = sin_a * cos_c + cos_a * sin_c
            for c in range(0, 8, 2):
                cosines, sines = [], []
                for d in (c, c + 1):
                    cos_r, sin_r = cos_ac[d : d + 1], sin_ac[d : d + 1]
                    cosines.append(cos_r * cos_b - sin_r * sin_b)
                    sines.append(sin_r * cos_b + cos_r * sin_b)
                store(i, 64 * a + 8 * c, jnp.concatenate(cosines, 0), jnp.concatenate(sines, 0))
        return carry

    lax.fori_loop(0, period // width, columns, 0)


def shifted(block, axis):
    size = block.shape[axis]
    return [pltpu.roll(block, shift % size, axis) for shift in (2, 1, -1, -2)]


def second_diff(block, rows, cols):
    ends = rows[0] + rows[3] + cols[0] + cols[3]
    near = rows[1] + rows[2] + cols[1] + cols[2]
    return (16.0 * near - ends - 60.0 * block) * (1.0 / 12.0)


def first_diff(moved):
    return ((moved[0] - moved[3]) + 8.0 * (moved[2] - moved[1])) * (1.0 / 12.0)


def kernel(
    substeps,
    n_row,
    n_col,
    height_in,
    rigid_in,
    adhes_in,
    force_in,
    new_out,
    wave_ref,
    height_ref,
    rigid_ref,
    adhes_ref,
    force_ref,
    new_ref,
    cosx_ref,
    sinx_ref,
    cosy_ref,
    siny_ref,
    surf,
    curv,
    extra,
    side_send,
    side_recv,
    edge_send,
    edge_recv,
    table_x,
    table_y,
    vel,
    modes,
    side_ssem,
    side_rsem,
    edge_ssem,
    edge_rsem,
    vel_ssem,
    vel_rsem,
    mode_ssem,
    mode_rsem,
    load_sem,
    out_sem,
):
    rows, cols = height_ref.shape
    chunks = cols // LANES
    wide = cols + LANES
    me_r = lax.axis_index("row")
    me_c = lax.axis_index("col")
    down = lax.rem(me_r + 1, n_row)
    up = lax.rem(me_r + n_row - 1, n_row)
    right = lax.rem(me_c + 1, n_col)
    left = lax.rem(me_c + n_col - 1, n_col)
    sibling = me_c + 1 - 2 * lax.rem(me_c, 2)
    mesh_ids = pl.DeviceIdType.MESH

    loads = [
        pltpu.make_async_copy(src, dst, load_sem.at[i])
        for i, (src, dst) in enumerate(
            (
                (height_in, height_ref),
                (rigid_in, rigid_ref),
                (adhes_in, adhes_ref),
                (force_in, force_ref),
            )
        )
    ]
    for copy in loads:
        copy.start()

    barrier = pltpu.get_barrier_semaphore()
    for target in (down, up):
        pl.semaphore_signal(barrier, inc=1, device_id={"row": target}, device_id_type=mesh_ids)
    for off in range(1, n_col):
        pl.semaphore_signal(
            barrier,
            inc=1,
            device_id={"col": lax.rem(me_c + off, n_col)},
            device_id_type=mesh_ids,
        )

    def send(src, dst, ssem, rsem, where):
        return pltpu.make_async_remote_copy(
            src_ref=src,
            dst_ref=dst,
            send_sem=ssem,
            recv_sem=rsem,
            device_id=where,
            device_id_type=mesh_ids,
        )

    pack_rows = 32
    for copy in loads:
        copy.wait()

    def pack(i, carry):
        at = pl.ds(pl.multiple_of(i * pack_rows, pack_rows), pack_rows)
        slot = lax.broadcasted_iota(jnp.int32, (pack_rows, LANES), 1) // HALO
        for side in range(2):
            lanes = slice(0, LANES) if side == 0 else slice(cols - LANES, cols)
            base = 0 if side == 0 else HALO
            first = height_ref[at, lanes]
            coarse = first.astype(jnp.bfloat16).astype(jnp.float32)
            fields = [coarse, first - coarse, rigid_ref[at, lanes], adhes_ref[at, lanes]]
            for s in range(substeps):
                fields.append(force_ref[s, at, lanes].astype(jnp.float32))
            tile = jnp.zeros((pack_rows, LANES), jnp.float32)
            for f, field in enumerate(fields):
                turn = (f * HALO + base) % LANES
                moved = pltpu.roll(field, turn, 1) if turn else field
                tile = jnp.where(slot == f, moved, tile)
            side_send[side, at, :] = tile.astype(jnp.bfloat16)
        return carry

    lax.fori_loop(0, rows // pack_rows, pack, 0)
    pl.semaphore_wait(barrier, 2 + n_col - 1)

    sides = [
        send(side_send.at[k], side_recv.at[k], side_ssem.at[k], side_rsem.at[k], {"col": where})
        for k, where in ((0, left), (1, right))
    ]
    for copy in sides:
        copy.start()

    modes_here = table_x.shape[0] // 2

    def store_x(i, row, cosines, sines):
        lanes = pl.ds(pl.multiple_of(i * cols, cols), cols)
        table_x[row : row + 16, lanes] = cosines.astype(jnp.bfloat16)
        table_x[modes_here + row : modes_here + row + 16, lanes] = (-sines).astype(jnp.bfloat16)

    write_phases(me_r * modes_here, cosx_ref, sinx_ref)
    write_table(cosx_ref, sinx_ref, modes_here // 64, cols, store_x)

    for copy in sides:
        copy.wait_recv()

    def unpack(i, carry):
        at = pl.ds(pl.multiple_of(i * pack_rows, pack_rows), pack_rows)
        lane = lax.broadcasted_iota(jnp.int32, (pack_rows, LANES), 1)
        after = side_recv[0, at, :].astype(jnp.float32)
        before = side_recv[1, at, :].astype(jnp.float32)
        got = []
        for f in range(4 + substeps):
            turn_a = (-f * HALO) % LANES
            turn_b = (-HALO - f * HALO) % LANES
            a = pltpu.roll(after, turn_a, 1) if turn_a else after
            b = pltpu.roll(before, turn_b, 1) if turn_b else before
            got.append(jnp.where(lane < LANES // 2, a, b))
        inside = pl.ds(pl.multiple_of(i * pack_rows + PAD, 16), pack_rows)
        surf[inside, 0:cols] = height_ref[at, :]
        surf[inside, cols:wide] = got[0] + got[1]
        for f in range(2, 4 + substeps):
            extra[f - 2, at, :] = got[f]
        return carry

    lax.fori_loop(0, rows // pack_rows, unpack, 0)

    def edge_copies(s):
        return [
            send(
                edge_send.at[s, k],
                edge_recv.at[s, k],
                edge_ssem.at[s, k],
                edge_rsem.at[s, k],
                {"row": where},
            )
            for k, where in ((0, up), (1, down))
        ]

    def send_edges(s):
        edge_send[s, 0] = surf[PAD : PAD + 8, :]
        edge_send[s, 1] = surf[PAD + rows - 8 : PAD + rows, :]
        copies = edge_copies(s)
        for copy in copies:
            copy.start()
        return copies

    def bend(start, count):
        block = surf[pl.ds(start - 8, count + 16), :]
        moved_rows = [m[8:-8] for m in shifted(block, 0)]
        middle = block[8:-8]
        moved_cols = shifted(middle, 1)
        slope_r = first_diff(moved_rows)
        slope_c = first_diff(moved_cols)
        metric = 1.0 + (slope_r * slope_r + slope_c * slope_c)
        inverse = lax.rsqrt(metric)
        curv[pl.ds(start, count), :] = (
            second_diff(middle, moved_rows, moved_cols) * (inverse * inverse * inverse)
        )

    def advance(start, count, s):
        inside = pl.ds(start + PAD, count)
        at = pl.ds(start, count)
        block = curv[pl.ds(start + PAD - 8, count + 16), :]
        moved_rows = [m[8:-8] for m in shifted(block, 0)]
        middle = block[8:-8]
        lap = second_diff(middle, moved_rows, shifted(middle, 1))
        rigid = jnp.concatenate([rigid_ref[at, :], extra[0, at, :]], 1)
        adhes = jnp.concatenate([adhes_ref[at, :], extra[1, at, :]], 1)
        noise = jnp.concatenate([force_ref[s, at, :].astype(jnp.float32), extra[2 + s, at, :]], 1)
        center = surf[inside, :]
        binding = adhes * center * jnp.exp(-0.5 * center * center)
        result = center + step_size * (noise - rigid * lap - binding)
        if s < substeps - 1:
            surf[inside, :] = result
        else:
            final = result[:, 0:cols]
            new_ref[at, :] = final
            speed = ((final - height_ref[at, :]) * (1.0 / (substeps * step_size))).astype(
                jnp.bfloat16
            )
            for q in range(chunks):
                vel[q, pl.ds(pl.multiple_of(me_r * rows, rows) + start, count), :] = speed[
                    :, q * LANES : (q + 1) * LANES
                ]

    inner = rows - 32
    strip = next(k for k in (96, 48, 32, 16) if inner % k == 0)

    def send_own(start, count):
        for q in range(chunks):
            part = vel.at[q, pl.ds(pl.multiple_of(me_r * rows + start, 16), count), :]
            for way, where in ((0, down), (1, up)):

                @pl.when(me_r + 1 < n_row if way == 0 else me_r > 0)
                def _(part=part, way=way, where=where, q=q):
                    sems = (way, 0, q)
                    send(
                        part, part, vel_ssem.at[sems], vel_rsem.at[sems], {"row": where}
                    ).start()

    pending = send_edges(0)
    edges = list(pending)
    for s in range(substeps):

        def bend_strip(i, carry):
            bend(pl.multiple_of(PAD + 16 + i * strip, 16), strip)
            return carry

        def advance_strip(i, carry, s=s):
            advance(pl.multiple_of(16 + i * strip, 16), strip, s)
            return carry

        lax.fori_loop(0, inner // strip, bend_strip, 0)
        for copy in pending:
            copy.wait_recv()
        surf[PAD - 8 : PAD, :] = edge_recv[s, 1]
        surf[PAD + rows : PAD + rows + 8, :] = edge_recv[s, 0]
        bend(PAD - 8, 24)
        bend(PAD + rows - 16, 24)
        advance(0, 16, s)
        advance(rows - 16, 16, s)
        if s < substeps - 1:
            pending = send_edges(s + 1)
            edges += pending
        if s < substeps - 1:
            lax.fori_loop(0, inner // strip, advance_strip, 0)
            continue
        some = inner // strip * 2 // 5
        lax.fori_loop(0, some, advance_strip, 0)
        cut = 16 + some * strip
        send_own(0, cut)
        lax.fori_loop(some, inner // strip, advance_strip, 0)
        send_own(cut, rows - cut)

    def vel_copy(way, distance, q):
        owner = me_r - distance if way == 0 else me_r + distance
        where = down if way == 0 else up
        part = vel.at[q, pl.ds(pl.multiple_of(owner * rows, rows), rows), :]
        sems = (way, distance, q)
        return send(part, part, vel_ssem.at[sems], vel_rsem.at[sems], {"row": where})

    def can_send(way, distance):
        if way == 0:
            return jnp.logical_and(me_r >= distance, me_r + 1 < n_row)
        return jnp.logical_and(me_r + distance < n_row, me_r > 0)

    def has_block(way, distance):
        return me_r >= distance if way == 0 else me_r + distance < n_row

    def vel_arrival(way, distance, q):
        owner = me_r - distance if way == 0 else me_r + distance
        part = vel.at[q, pl.ds(pl.multiple_of(owner * rows, rows), rows), :]
        sems = (way, distance - 1, q)
        where = down if way == 0 else up
        return send(part, part, vel_ssem.at[sems], vel_rsem.at[sems], {"row": where})

    def push(way, distance, q):
        @pl.when(can_send(way, distance))
        def _():
            vel_copy(way, distance, q).start()

    result_out = pltpu.make_async_copy(new_ref, new_out, out_sem)
    result_out.start()

    def store_y(i, row, cosines, sines):
        lanes = pl.ds(pl.multiple_of(i * LANES, LANES), LANES)
        for q in range(chunks):
            part = slice(q * LANES, (q + 1) * LANES)
            table_y[q, row : row + 16, lanes] = cosines[:, part].astype(jnp.bfloat16)
            table_y[q, cols + row : cols + row + 16, lanes] = sines[:, part].astype(jnp.bfloat16)

    write_phases(me_c * cols, cosy_ref, siny_ref)
    write_table(cosy_ref, siny_ref, cols // 64, cols, store_y)

    def mode_part(q, owner):
        return modes.at[q, :, pl.ds(pl.multiple_of(owner * LANES, LANES), LANES)]

    def mode_copy(q, owner, slot, where):
        part = mode_part(q, owner)
        return send(part, part, mode_ssem.at[q, slot], mode_rsem.at[q, slot], {"col": where})

    pairs = n_col // 2
    for q in range(chunks):
        for distance in range(1, n_row):
            for way in range(2):

                @pl.when(has_block(way, distance))
                def _(way=way, distance=distance, q=q):
                    vel_arrival(way, distance, q).wait_recv()

                if distance < n_row - 1:
                    push(way, distance, q)
        result = jnp.dot(table_x[...], vel[q], preferred_element_type=jnp.float32)
        mine = pl.ds(pl.multiple_of(me_c * LANES, LANES), LANES)
        modes[q, :, mine] = result.astype(jnp.bfloat16)
        for off in range(1, pairs):
            mode_copy(q, me_c, pairs - 1 + off, lax.rem(me_c + 2 * off, n_col)).start()
        mode_copy(q, me_c, 0, sibling).start()

    for q in range(chunks):
        for off in range(1, pairs):
            owner = lax.rem(me_c + n_col - 2 * off, n_col)
            mode_copy(q, owner, pairs - 1 + off, sibling).wait_recv()
            mode_copy(q, owner, off, sibling).start()
        mode_copy(q, sibling, 0, sibling).wait_recv()
        for off in range(1, pairs):
            owner = lax.rem(sibling + n_col - 2 * off, n_col)
            mode_copy(q, owner, off, sibling).wait_recv()
        terms = lax.dot_general(
            table_y[q], modes[q], (((1,), (1,)), ((), ())), preferred_element_type=jnp.float32
        )
        k = modes_here
        real = terms[:cols, :k] + terms[cols:, k:]
        imag = terms[:cols, k:] - terms[cols:, :k]
        if q == 0:
            wave_ref[:, :k] = real
            wave_ref[:, k:] = imag
        else:
            wave_ref[:, :k] += real
            wave_ref[:, k:] += imag

    result_out.wait()
    for copy in sides + edges:
        copy.wait_send()
    for q in range(chunks):
        for distance in range(n_row - 1):
            for way in range(2):

                @pl.when(can_send(way, distance))
                def _(way=way, distance=distance, q=q):
                    vel_copy(way, distance, q).wait_send()

        for off in range(1, pairs):
            mode_copy(q, me_c, pairs - 1 + off, lax.rem(me_c + 2 * off, n_col)).wait_send()
            mode_copy(q, me_c, off, sibling).wait_send()
        mode_copy(q, me_c, 0, sibling).wait_send()


def on_device(height, rigidity, adhesion, forcing):
    rows, cols = height.shape
    substeps = forcing.shape[0]
    n_row = lax.axis_size("row")
    n_col = lax.axis_size("col")
    full_rows, full_cols = rows * n_row, cols * n_col
    local_modes = full_rows // 2 // n_row
    chunks = cols // LANES
    pairs = n_col // 2
    wide = cols + LANES
    row_at = lax.axis_index("row") * local_modes
    col_at = lax.axis_index("col") * cols
    rows_x = 16 + -(-local_modes // 512) * 8
    rows_y = 16 + -(-cols // 512) * 8
    f32, bf16 = jnp.float32, jnp.bfloat16
    dma = pltpu.SemaphoreType.DMA
    hbm = pl.BlockSpec(memory_space=pltpu.HBM)
    vmem = pl.BlockSpec(memory_space=pltpu.VMEM)
    new_height, waves = pl.pallas_call(
        functools.partial(kernel, substeps, n_row, n_col),
        out_shape=(
            jax.ShapeDtypeStruct((rows, cols), f32),
            jax.ShapeDtypeStruct((cols, 2 * local_modes), f32),
        ),
        in_specs=[hbm] * 4,
        out_specs=(hbm, vmem),
        scratch_shapes=[
            pltpu.VMEM((rows, cols), f32),
            pltpu.VMEM((rows, cols), f32),
            pltpu.VMEM((rows, cols), f32),
            pltpu.VMEM((substeps, rows, cols), bf16),
            pltpu.VMEM((rows, cols), f32),
            pltpu.VMEM((rows_x, full_rows), f32),
            pltpu.VMEM((rows_x, full_rows), f32),
            pltpu.VMEM((rows_y, full_cols), f32),
            pltpu.VMEM((rows_y, full_cols), f32),
            pltpu.VMEM((rows + 2 * PAD, wide), f32),
            pltpu.VMEM((rows + 2 * PAD, wide), f32),
            pltpu.VMEM((2 + substeps, rows, LANES), f32),
            pltpu.VMEM((2, rows, LANES), bf16),
            pltpu.VMEM((2, rows, LANES), bf16),
            pltpu.VMEM((substeps, 2, 8, wide), f32),
            pltpu.VMEM((substeps, 2, 8, wide), f32),
            pltpu.VMEM((2 * local_modes, full_rows), bf16),
            pltpu.VMEM((chunks, 2 * cols, n_col * LANES), bf16),
            pltpu.VMEM((chunks, full_rows, LANES), bf16),
            pltpu.VMEM((chunks, 2 * local_modes, n_col * LANES), bf16),
            dma((2,)),
            dma((2,)),
            dma((substeps, 2)),
            dma((substeps, 2)),
            dma((2, n_row - 1, chunks)),
            dma((2, n_row - 1, chunks)),
            dma((chunks, 2 * pairs - 1)),
            dma((chunks, 2 * pairs - 1)),
            dma((4,)),
            dma,
        ],
        compiler_params=pltpu.CompilerParams(
            collective_id=0, has_side_effects=True, vmem_limit_bytes=127 * 512 * 1024
        ),
    )(height, rigidity, adhesion, forcing)
    wave_y = col_at + lax.iota(jnp.int32, cols)
    signed = jnp.where(wave_y < full_cols // 2, wave_y, wave_y - full_cols)
    angle_y = signed.astype(f32) * (2.0 * math.pi / full_cols)
    wave_x = row_at + lax.iota(jnp.int32, local_modes)
    angle_x = wave_x.astype(f32) * (2.0 * math.pi / full_rows)
    squared = angle_y[:, None] * angle_y[:, None] + angle_x[None, :] * angle_x[None, :]
    mobility = 1.0 / (2.0 * jnp.sqrt(squared + wave_floor)) / math.sqrt(full_rows * full_cols)
    spectrum = waves.reshape(cols, 2, local_modes) * mobility[:, None, :]
    return (new_height, spectrum)


def solution(mesh):
    in_specs = (
        P(("groups", "row"), "col"),
        P(("groups", "row"), "col"),
        P(("groups", "row"), "col"),
        P(None, ("groups", "row"), "col"),
    )
    out_specs = (P(("groups", "row"), "col"), P(("groups", "col"), None, "row"))
    return jax.shard_map(
        on_device, mesh=mesh, in_specs=in_specs, out_specs=out_specs, check_vma=False
    )
```
